32 devices in a mesh: leaf: 8 (over y, x, core), probe: 4 (over z).
Axes of the slice: x: 2, y: 2, z: 4, core: 2. Of those that a mesh axis runs over, the one named last changes fastest.
Arguments:
- child_updates: bfloat16 [256, 512, 512], P('leaf'), may hold values from -0.25 to 0.25
- child_probes: bfloat16 [256, 131072], P('probe', 'leaf'), may hold values from -6 to 6
- child_dest: int32 [1024, 1], P('leaf'), may hold values from 0 to 7; in each aligned block of 128 rows (0 to 127, 128 to 255, ...) at most 32 rows name the same one
- child_rows: int32 [1024, 128], P('leaf'), may hold values from 0 to 2047
- parent_blocks: bfloat16 [512, 128, 128], P('leaf'), may hold values from -0.5 to 0.5
- coupling: int32 [512, 2], P('leaf'), may hold values from 0 to 15
- parent_probes: bfloat16 [256, 16384], P('probe', 'leaf'), may hold values from -6 to 6
- sketch: float32 [256, 128], P('probe'), may hold values from -0.375 to 0.375
- rank_one: int32 [8], P('leaf'), may hold values from 96 to 128, as said below
- rank_two: int32 [4], replicated, may hold values from 96 to 128, as said below
- rank_three: int32 [2], replicated, may hold values from 96 to 128, as said below
Outputs:
- basis_one: float32 [16384, 128], P(('leaf', 'probe'))
- basis_two: float32 [1024, 128], P('leaf')
- basis_three: float32 [1024, 128], P('leaf')
- top_sample: float32 [256, 1024], P('probe', 'leaf')
The draws below stay inside these ranges and needn't reach their ends.
Inputs may be any that keep to these rules, and one draw needn't show every extreme that they name: `child_dest`: among the row blocks of one front group, no parent front is named by more than 32 blocks, and some parent front is named by exactly 32. `rank_one`: one node has rank 128. `rank_two`: one node has rank 128. `rank_three`: one node has rank 128.
All inputs are finite; a program needn't handle non-finite values.
Results may differ from the reference program's by a relative error of at most 0.0065.
Values may be sent and summed in bfloat16 or wider, within the bound.
A program may use at most 192 MiB of HBM per device.

```python
import math
import jax
import jax.numpy as jnp
import numpy as np
from jax import lax

PROBES = 256
RANK = 128
RB = 128
CB = 512
PF = 2048
NZB = 64
CH = 32
FRONTS = 8
PAIRS = 4
QUADS = 2
CHB = 128
CAP = 32
PB = 16
CHILDREN = 256


def rank_draw(key, count):
    values = jax.random.randint(key, (count,), 3 * RANK // 4, RANK + 1)
    place = jax.random.randint(jax.random.fold_in(key, 7), (), 0, count)
    return values.at[place].set(RANK).astype(jnp.int32)


def draw_rank_one(key, part):
    return rank_draw(jax.random.fold_in(key, 11), FRONTS)


def draw_rank_two(key, part):
    return rank_draw(jax.random.fold_in(key, 13), PAIRS)


def draw_rank_three(key, part):
    return rank_draw(jax.random.fold_in(key, 17), QUADS)


def set_ends(values, key, least, top_value):
    extent = values.shape
    spot = [jax.random.randint(jax.random.fold_in(key, axis), (), 0, extent[axis]) for axis in range(len(extent))]
    values = values.at[tuple(spot)].set(least)
    longest = extent.index(max(extent))
    spot[longest] = (spot[longest] + 1) % extent[longest]
    return values.at[tuple(spot)].set(top_value)


def steps_of(own_key, extent, cuts, low, high):
    gain = 1.0
    for axis_at, shards_of in cuts:
        draws = jax.random.uniform(jax.random.fold_in(jax.random.fold_in(own_key, 6), axis_at), (shards_of,), jnp.float32, low / len(cuts), high / len(cuts))
        gain = gain * jnp.repeat(jnp.exp(draws), extent[axis_at] // shards_of).reshape((-1,) + (1,) * (len(extent) - 1 - axis_at))
    return gain


def routed_block(rng, own, number, rows, amount, top, limit, lean):
    sequence = jax.random.permutation(rng, amount)
    crowded, ordinary = load_shares(amount, rows * top, limit, lean, True), load_shares(amount, rows * top, limit, lean, False)
    places = jnp.arange(amount)

    def named(tallies, turn):
        used = int((tallies > 0).sum())
        fixed = max(1, used // 4)
        moved = fixed + (places - fixed + turn * (used - fixed)) % max(1, amount - fixed)
        return jnp.zeros((amount,), jnp.int32).at[sequence[jnp.where(places < fixed, places, moved)]].set(jnp.asarray(tallies, jnp.int32))

    tallies = jnp.where(number % 4 == 0, named(crowded, number // 4), named(ordinary, number - number // 4 - 1))
    mixed = jax.random.permutation(jax.random.fold_in(own, 3), amount)
    donor, sink = mixed[0:amount // 2 * 2:2], mixed[1:amount // 2 * 2:2]
    room = jnp.minimum(tallies[donor] - 1, limit - tallies[sink]) // 2
    room = jnp.where((donor == sequence[0]) | (sink == sequence[0]) | (tallies[sink] == 0), 0, jnp.maximum(room, 0))
    moved = jax.random.randint(jax.random.fold_in(own, 4), (amount // 2,), 0, 1 << 20) % (room + 1)
    tallies = tallies.at[donor].add(-moved).at[sink].add(moved)
    members = jnp.searchsorted(jnp.cumsum(tallies), jnp.arange(rows * top), side="right").astype(jnp.int32)
    grid = members.reshape(top, rows).T
    grid = grid[jax.random.permutation(jax.random.fold_in(own, 1), rows)]
    turn = jax.random.randint(jax.random.fold_in(own, 2), (rows, 1), 0, top)
    return jnp.take_along_axis(grid, (jnp.arange(top)[None, :] + turn) % top, axis=1)


def load_shares(number_of, total, limit, slope, full):
    weights = [(1 << 20) // math.isqrt(standing ** slope) + 1 for standing in range(1, number_of + 1)]
    largest = limit if full else min(limit, max(-(-total // number_of), total * weights[0] // sum(weights)))
    least = 1 if total - largest >= number_of - 1 else 0
    holding, surplus = [largest] + [least] * (number_of - 1), total - largest - least * (number_of - 1)
    while surplus > 0:
        candidates = [i for i in range(1, number_of) if holding[i] < largest] or [i for i in range(1, number_of) if holding[i] < limit]
        mass, left = sum([weights[i] for i in candidates]), surplus
        for i in candidates:
            more = min(limit - holding[i], max(1, left * weights[i] // mass), surplus)
            holding[i] = holding[i] + more
            surplus = surplus - more
    return np.array(holding)


def bell_draw(rng, extent, deviation, limit, split=(), kind=jnp.bfloat16):
    array = jax.random.normal(rng, extent, jnp.float32) * deviation
    if len(split) > 0:
        array = steps_of(rng, extent, split, -0.22, 0.18) * array
    return jnp.clip(array, min=-limit, max=limit).astype(kind)


def setup_inputs(seed: int = 0) -> dict:
    arg_keys = jax.random.split(jax.random.key(seed), 12)
    child_updates = bell_draw(arg_keys[0], (CHILDREN, CB, CB), CB ** -0.5, 0.25, ((0, 8),))
    child_probes = bell_draw(arg_keys[1], (PROBES, CHILDREN * CB), 1.0, 6.0, ((0, 4), (1, 8)))
    child_dest_keys = jax.random.split(jax.random.fold_in(arg_keys[2], 1), (FRONTS * CHB) // CHB)
    child_dest_turns = jax.random.permutation(jax.random.fold_in(arg_keys[2], 3), (FRONTS * CHB) // CHB)
    child_dest = jax.vmap(lambda own, number: routed_block(jax.random.fold_in(arg_keys[2], 2), own, number, CHB, FRONTS, 1, CAP, 2))(child_dest_keys, child_dest_turns).reshape((FRONTS * CHB, 1))
    child_rows = set_ends(jax.random.randint(arg_keys[3], (FRONTS * CHB, RB), 0, PF), jax.random.fold_in(arg_keys[3], 1), 0, PF - 1).astype(jnp.int32)
    parent_blocks = bell_draw(arg_keys[4], (FRONTS * NZB, RB, RB), RB ** -0.5, 0.5, ((0, 8),))
    coupling = set_ends(jax.random.randint(arg_keys[5], (FRONTS * NZB, 2), 0, PB), jax.random.fold_in(arg_keys[5], 1), 0, PB - 1).astype(jnp.int32)
    parent_probes = bell_draw(arg_keys[6], (PROBES, FRONTS * PF), 1.0, 6.0, ((0, 4), (1, 8)))
    sketch = bell_draw(arg_keys[7], (PROBES, RANK), PROBES ** -0.5, 0.375, ((0, 4),), jnp.float32)
    rank_one = draw_rank_one(jax.random.fold_in(arg_keys[11], 71), 0)
    rank_two = draw_rank_two(jax.random.fold_in(arg_keys[11], 71), 0)
    rank_three = draw_rank_three(jax.random.fold_in(arg_keys[11], 71), 0)
    return dict(child_updates=child_updates, child_probes=child_probes, child_dest=child_dest, child_rows=child_rows, parent_blocks=parent_blocks, coupling=coupling, parent_probes=parent_probes, sketch=sketch, rank_one=rank_one, rank_two=rank_two, rank_three=rank_three)


highest = lax.Precision.HIGHEST

def chol_basis(sketched, rank_limit):
    gram_matrix = jnp.dot(sketched.T, sketched, precision=highest)
    factor = jnp.linalg.cholesky(gram_matrix)
    orthonormal = lax.linalg.triangular_solve(factor, sketched, left_side=False, lower=True, transpose_a=True)
    columns = jnp.arange(sketched.shape[1], dtype=jnp.int32)
    return jnp.where(columns[None, :] < rank_limit, orthonormal, jnp.zeros_like(orthonormal))

def merge_level(samples, sketch, ranks):
    stacked = jnp.concatenate([samples[0::2], samples[1::2]], axis=2)
    sketched = jnp.einsum('npr,ps->nrs', stacked, sketch, precision=highest)
    merged = jax.vmap(chol_basis)(sketched, ranks)
    passed = jnp.einsum('npr,nrs->nps', stacked, merged, precision=highest)
    return (merged, passed)

def reference(child_updates, child_probes, child_dest, child_rows, parent_blocks, coupling, parent_probes, sketch, rank_one, rank_two, rank_three):
    fronts_all = rank_one.shape[0]
    updates = child_updates.reshape(fronts_all, CH, CB // RB, RB, CB)
    probes_kids = child_probes.reshape(PROBES, fronts_all, CH, CB)
    targets = child_dest.reshape(fronts_all, CHB)
    row_maps = child_rows.reshape(fronts_all, CHB, RB)

    def add_group(extended, group):
        probe_block = lax.dynamic_index_in_dim(probes_kids, group, 1, keepdims=False).astype(jnp.float32)
        update_block = lax.dynamic_index_in_dim(updates, group, 0, keepdims=False).astype(jnp.float32)
        sampled = jnp.einsum('pck,cbik->cbpi', probe_block, update_block).astype(jnp.bfloat16)
        sampled = sampled.reshape(CHB, PROBES, RB)
        target_rows = lax.dynamic_index_in_dim(targets, group, 0, keepdims=False)
        local_rows = lax.dynamic_index_in_dim(row_maps, group, 0, keepdims=False)
        global_rows = (target_rows[:, None] * PF + local_rows).reshape(-1)
        values = jnp.moveaxis(sampled, 1, 0).reshape(PROBES, CHB * RB).astype(jnp.float32)
        return (extended.at[:, global_rows].add(values), None)
    extended, _ = lax.scan(add_group, jnp.zeros((PROBES, fronts_all * PF), jnp.float32), jnp.arange(fronts_all, dtype=jnp.int32))
    blocks_all = parent_blocks.reshape(fronts_all, NZB, RB, RB)
    pattern = coupling.reshape(fronts_all, NZB, 2)
    probes_front = jnp.moveaxis(parent_probes.reshape(PROBES, fronts_all, PB, RB), 1, 0)

    def one_front(inputs):
        block_set, pattern_set, probe_set = inputs
        picked = jnp.take(probe_set, pattern_set[:, 1], axis=1).astype(jnp.float32)
        product = jnp.einsum('eik,pek->pei', block_set.astype(jnp.float32), picked)
        initial = jnp.zeros((PROBES, PB, RB), jnp.float32).at[:, pattern_set[:, 0]].add(product)
        return initial.reshape(PROBES, PF)
    initial_all = lax.map(one_front, (blocks_all, pattern, probes_front))
    sample_all = initial_all + jnp.moveaxis(extended.reshape(PROBES, fronts_all, PF), 1, 0)

    def level_one(sample_front, rank_limit):
        sketched = jnp.einsum('pr,ps->rs', sample_front, sketch, precision=highest)
        basis_front = chol_basis(sketched, rank_limit)
        return (basis_front, jnp.dot(sample_front, basis_front, precision=highest))
    basis_all, passed_one = jax.vmap(level_one)(sample_all, rank_one)
    merged_two, passed_two = merge_level(passed_one, sketch, rank_two)
    merged_three, passed_three = merge_level(passed_two, sketch, rank_three)
    basis_one = basis_all.reshape(fronts_all * PF, RANK)
    basis_two = merged_two.reshape(fronts_all * RANK, RANK)
    basis_three = jnp.repeat(merged_three.reshape(fronts_all // 2, RANK, RANK), 2, axis=0).reshape(fronts_all * RANK, RANK)
    top_sample = jnp.moveaxis(jnp.repeat(passed_three, 4, axis=0), 0, 1).reshape(PROBES, fronts_all * RANK)
    return (basis_one, basis_two, basis_three, top_sample)
```

```python
import functools
import jax
import jax.numpy as jnp
from jax import lax
from jax.experimental import pallas as pl
from jax.experimental.pallas import tpu as pltpu
from jax.sharding import PartitionSpec as P

highest = lax.Precision.HIGHEST
WIDE = 256
PANEL = 16


def dot(a, b, ca, cb, precision=None):
    return lax.dot_general(
        a, b, (((ca,), (cb,)), ((), ())), precision=precision, preferred_element_type=jnp.float32
    )


def partner_of(block, axis, stride):
    count = lax.axis_size(axis)
    route = [(i, i ^ (1 << stride)) for i in range(count)]
    return lax.ppermute(block, axis, route)


def sample_kernel(me_ref, dest_ref, coup_ref, upd_ref, probe_ref, rows_ref, blk_ref, pp_ref,
                  part_ref, own_ref, acc):
    step = pl.program_id(0)
    me = me_ref[0]
    high_count = acc.shape[1]
    row_blocks = rows_ref.shape[1]
    width = rows_ref.shape[2]

    @pl.when(step == 0)
    def _():
        acc[...] = jnp.zeros_like(acc)

    sampled = dot(probe_ref[...], upd_ref[0], 1, 1).astype(jnp.bfloat16)
    for b in range(row_blocks):
        rows = rows_ref[0, b : b + 1, :]
        high = lax.shift_right_logical(rows, 8)
        low = lax.bitwise_and(rows, WIDE - 1)
        spots = lax.broadcasted_iota(jnp.int32, (WIDE, width), 0)
        low_hot = jnp.where(spots == low, 1.0, 0.0).astype(jnp.bfloat16)
        part = sampled[:, b * width : (b + 1) * width]
        left = jnp.concatenate(
            [part * jnp.where(high == h, 1.0, 0.0).astype(jnp.bfloat16) for h in range(high_count)], 0
        )
        spread = dot(left, low_hot, 1, 1).reshape(acc.shape[1:])
        f = dest_ref[step * row_blocks + b]
        acc[f] += spread
    per_step = blk_ref.shape[0]
    for e in range(per_step):
        q = coup_ref[2 * (step * per_step + e)]
        s = coup_ref[2 * (step * per_step + e) + 1]
        picked = pp_ref[:, pl.ds(pl.multiple_of(s * width, width), width)]
        lane = pl.multiple_of((q % 2) * width, width)
        acc[me, q // 2, :, pl.ds(lane, width)] += dot(picked, blk_ref[e], 1, 1)

    @pl.when(step == pl.num_programs(0) - 1)
    def _():
        part_ref[...] = acc[...].astype(jnp.bfloat16)
        own_ref[...] = acc[me]


def local_samples(me, child_updates, child_probes, child_dest, child_rows, parent_blocks, coupling,
                  parent_probes, leaf_count):
    kids, order, _ = child_updates.shape
    probes = child_probes.shape[0]
    width = child_rows.shape[1]
    per_kid = order // width
    front_rows = parent_probes.shape[1]
    entries = parent_blocks.shape[0] // kids
    high = front_rows // WIDE
    rows = child_rows.reshape(kids, per_kid, width)
    grid_spec = pltpu.PrefetchScalarGridSpec(
        num_scalar_prefetch=3,
        grid=(kids,),
        in_specs=[
            pl.BlockSpec((1, order, order), lambda c, *_: (c, 0, 0)),
            pl.BlockSpec((probes, order), lambda c, *_: (0, c)),
            pl.BlockSpec((1, per_kid, width), lambda c, *_: (c, 0, 0)),
            pl.BlockSpec((entries, width, width), lambda c, *_: (c, 0, 0)),
            pl.BlockSpec((probes, front_rows), lambda c, *_: (0, 0)),
        ],
        out_specs=[
            pl.BlockSpec((leaf_count, high, probes, WIDE), lambda c, *_: (0, 0, 0, 0)),
            pl.BlockSpec((high, probes, WIDE), lambda c, *_: (0, 0, 0)),
        ],
        scratch_shapes=[pltpu.VMEM((leaf_count, high, probes, WIDE), jnp.float32)],
    )
    return pl.pallas_call(
        sample_kernel,
        grid_spec=grid_spec,
        out_shape=[
            jax.ShapeDtypeStruct((leaf_count, high, probes, WIDE), jnp.bfloat16),
            jax.ShapeDtypeStruct((high, probes, WIDE), jnp.float32),
        ],
        compiler_params=pltpu.CompilerParams(vmem_limit_bytes=56 * 1024 * 1024),
    )(me[None], child_dest.reshape(-1), coupling.reshape(-1), child_updates, child_probes, rows,
      parent_blocks, parent_probes)


def inverse_factor(work, done, gram):
    n = gram.shape[0]
    eye = lax.broadcasted_iota(jnp.int32, (n, n), 0) == lax.broadcasted_iota(jnp.int32, (n, n), 1)
    work[:, :n] = gram
    work[:, n:] = jnp.where(eye, 1.0, 0.0)
    place = lax.broadcasted_iota(jnp.int32, (PANEL, 1), 0)
    for k in range(0, n, PANEL):
        panel = work[k : k + PANEL, :]
        for j in range(PANEL):
            column = panel[:, k + j : k + j + 1]
            scale = lax.rsqrt(column[j : j + 1, :])
            row = panel[j : j + 1, :] * scale
            weight = jnp.where(place > j, column * scale, 0.0)
            panel = jnp.where(place == j, row, panel - weight * row)
        done[k : k + PANEL, :] = panel
        if k + PANEL < n:
            work[...] -= dot(panel[:, :n], panel, 0, 0, highest)
    return done[:, n:]


def basis_kernel(rank_ref, gram_ref, stack_ref, out_ref, work, done):
    inverse = inverse_factor(work, done, gram_ref[...])
    result = dot(stack_ref[...], inverse, 1, 1, highest)
    columns = lax.broadcasted_iota(jnp.int32, result.shape, 1)
    out_ref[...] = jnp.where(columns < rank_ref[0], result, 0.0)


def basis_apply(rank, gram, stack):
    n = gram.shape[0]
    return pl.pallas_call(
        basis_kernel,
        in_specs=[
            pl.BlockSpec(memory_space=pltpu.SMEM),
            pl.BlockSpec(memory_space=pltpu.VMEM),
            pl.BlockSpec(memory_space=pltpu.VMEM),
        ],
        out_specs=pl.BlockSpec(memory_space=pltpu.VMEM),
        out_shape=jax.ShapeDtypeStruct(stack.shape, jnp.float32),
        scratch_shapes=[pltpu.VMEM((n, 2 * n), jnp.float32), pltpu.VMEM((n, 2 * n), jnp.float32)],
        compiler_params=pltpu.CompilerParams(vmem_limit_bytes=24 * 1024 * 1024),
    )(rank.reshape(1), gram, stack)


def merge(passed, bit, stride, sketch, rank):
    partner = partner_of(passed, "leaf", stride)
    stacked = jnp.where(
        bit == 0,
        jnp.concatenate([passed, partner], 1),
        jnp.concatenate([partner, passed], 1),
    )
    sketched = jnp.einsum("pr,ps->rs", stacked, sketch, precision=highest)
    gram = jnp.einsum("ra,rb->ab", sketched, sketched, precision=highest)
    crossed = jnp.dot(stacked, sketched, precision=highest)
    both = basis_apply(rank, gram, jnp.concatenate([sketched, crossed], 0))
    rows = sketched.shape[0]
    return both[:rows], both[rows:]


def on_device(
    child_updates,
    child_probes,
    child_dest,
    child_rows,
    parent_blocks,
    coupling,
    parent_probes,
    sketch,
    rank_one,
    rank_two,
    rank_three,
):
    leaf_count = lax.axis_size("leaf")
    probe_count = lax.axis_size("probe")
    leaf_index = lax.axis_index("leaf")
    probe_index = lax.axis_index("probe")
    probes, front_rows = parent_probes.shape
    rank_width = sketch.shape[1]
    sketch_all = lax.all_gather(sketch, "probe", axis=0, tiled=True)
    partial, own = local_samples(
        leaf_index, child_updates, child_probes, child_dest, child_rows, parent_blocks, coupling,
        parent_probes, leaf_count,
    )
    arrived = lax.all_to_all(partial, "leaf", 0, 0, tiled=True)
    others = jnp.arange(leaf_count) != leaf_index
    sample = own + jnp.sum(
        jnp.where(others[:, None, None, None], arrived.astype(jnp.float32), 0.0), axis=0
    )
    high = front_rows // WIDE
    share = sample.astype(jnp.bfloat16).reshape(probe_count, high // probe_count, probes, WIDE)
    share = lax.all_to_all(share, "probe", 0, 0, tiled=True)
    rows_mine = jnp.moveaxis(share, 1, 2).reshape(probe_count * probes, front_rows // probe_count)
    rows_mine = rows_mine.astype(jnp.float32)
    sketched = jnp.einsum("pr,ps->rs", rows_mine, sketch_all, precision=highest)
    gram = jnp.einsum("ra,rb->ab", sketched, sketched, precision=highest)
    crossed = jnp.dot(rows_mine, sketched, precision=highest)
    sums = jnp.concatenate([gram, crossed], 0)
    stride = 0
    while 1 << stride < probe_count:
        sums = sums + partner_of(sums, "probe", stride)
        stride += 1
    both = basis_apply(
        rank_one[0], sums[:rank_width], jnp.concatenate([sketched, sums[rank_width:]], 0)
    )
    own_basis, passed_one = both[: sketched.shape[0]], both[sketched.shape[0] :]
    pair_bit = leaf_index % 2
    merged_two, passed_two = merge(passed_one, pair_bit, 0, sketch_all, rank_two[leaf_index // 2])
    quad_bit = leaf_index // 2 % 2
    merged_three, passed_three = merge(passed_two, quad_bit, 1, sketch_all, rank_three[leaf_index // 4])
    basis_two = lax.dynamic_slice_in_dim(merged_two, pair_bit * rank_width, rank_width, 0)
    basis_three = lax.dynamic_slice_in_dim(merged_three, quad_bit * rank_width, rank_width, 0)
    top = lax.dynamic_slice_in_dim(passed_three, probe_index * probes, probes, 0)
    return (own_basis, basis_two, basis_three, top)


def solution(mesh):
    return jax.shard_map(
        on_device,
        mesh=mesh,
        in_specs=(
            P("leaf", None, None),
            P("probe", "leaf"),
            P("leaf", None),
            P("leaf", None),
            P("leaf", None, None),
            P("leaf", None),
            P("probe", "leaf"),
            P("probe", None),
            P("leaf"),
            P(),
            P(),
        ),
        out_specs=(
            P(("leaf", "probe"), None),
            P("leaf", None),
            P("leaf", None),
            P("probe", "leaf"),
        ),
        check_vma=False,
    )
```

```python
import functools
import jax
import jax.numpy as jnp
from jax import lax
from jax.experimental import pallas as pl
from jax.experimental.pallas import tpu as pltpu
from jax.sharding import PartitionSpec as P

highest = lax.Precision.HIGHEST
WIDE = 256
PANEL = 16
KIDS = 2


def dot(a, b, ca, cb, precision=None):
    return lax.dot_general(
        a, b, (((ca,), (cb,)), ((), ())), precision=precision, preferred_element_type=jnp.float32
    )


def partner_of(block, axis, stride):
    count = lax.axis_size(axis)
    route = [(i, i ^ (1 << stride)) for i in range(count)]
    return lax.ppermute(block, axis, route)


def gathered(block, axis):
    count = lax.axis_size(axis)
    index = lax.axis_index(axis)
    rows = block.shape[0]
    result = jnp.zeros((count * rows,) + block.shape[1:], block.dtype)
    result = lax.dynamic_update_slice_in_dim(result, block, index * rows, 0)
    for shift in range(1, count):
        came = lax.ppermute(block, axis, [(i, (i + shift) % count) for i in range(count)])
        source = (index - shift + count) % count
        result = lax.dynamic_update_slice_in_dim(result, came, source * rows, 0)
    return result


def sample_kernel(dest_ref, coup_ref, upd_ref, probe_ref, rows_ref, blk_ref, pp_ref,
                  send_ref, keep_ref, acc):
    step = pl.program_id(0)
    me = lax.axis_index("leaf")
    high_count = acc.shape[1]
    kids, row_blocks, width = rows_ref.shape
    order = upd_ref.shape[1]

    @pl.when(step == 0)
    def _():
        acc[...] = jnp.zeros_like(acc)

    spots = lax.broadcasted_iota(jnp.int32, (WIDE, width), 0)
    sampled = [
        dot(probe_ref[:, c * order : (c + 1) * order], upd_ref[c], 1, 1).astype(jnp.bfloat16)
        for c in range(kids)
    ]
    for c in range(kids):
        for b in range(row_blocks):
            rows = rows_ref[c, b : b + 1, :]
            high = lax.shift_right_logical(rows, 8)
            low = lax.bitwise_and(rows, WIDE - 1)
            low_hot = jnp.where(spots == low, 1.0, 0.0).astype(jnp.bfloat16)
            part = sampled[c][:, b * width : (b + 1) * width]
            left = jnp.concatenate(
                [
                    part * jnp.where(high == h, 1.0, 0.0).astype(jnp.bfloat16)
                    for h in range(high_count)
                ],
                0,
            )
            spread = dot(left, low_hot, 1, 1).reshape(acc.shape[1:])
            f = dest_ref[(step * kids + c) * row_blocks + b]
            acc[f] += spread
    per_step = blk_ref.shape[0]
    for e in range(per_step):
        q = coup_ref[2 * (step * per_step + e)]
        s = coup_ref[2 * (step * per_step + e) + 1]
        picked = pp_ref[:, pl.ds(pl.multiple_of(s * width, width), width)]
        lane = pl.multiple_of((q % 2) * width, width)
        acc[me, q // 2, :, pl.ds(lane, width)] += dot(picked, blk_ref[e], 1, 1)

    @pl.when(step == pl.num_programs(0) - 1)
    def _():
        bit = me % 2
        for i in range(send_ref.shape[0]):
            send_ref[i] = acc[2 * i + 1 - bit].astype(jnp.bfloat16)
            keep_ref[i] = acc[2 * i + bit]


def local_samples(child_updates, child_probes, child_dest, child_rows, parent_blocks, coupling,
                  parent_probes, leaf_count):
    kids, order, _ = child_updates.shape
    probes = child_probes.shape[0]
    width = child_rows.shape[1]
    per_kid = order // width
    front_rows = parent_probes.shape[1]
    steps = kids // KIDS
    entries = parent_blocks.shape[0] // steps
    high = front_rows // WIDE
    half = leaf_count // 2
    rows = child_rows.reshape(kids, per_kid, width)
    grid_spec = pltpu.PrefetchScalarGridSpec(
        num_scalar_prefetch=2,
        grid=(steps,),
        in_specs=[
            pl.BlockSpec((KIDS, order, order), lambda c, *_: (c, 0, 0)),
            pl.BlockSpec((probes, KIDS * order), lambda c, *_: (0, c)),
            pl.BlockSpec((KIDS, per_kid, width), lambda c, *_: (c, 0, 0)),
            pl.BlockSpec((entries, width, width), lambda c, *_: (c, 0, 0)),
            pl.BlockSpec((probes, front_rows), lambda c, *_: (0, 0)),
        ],
        out_specs=[
            pl.BlockSpec((half, high, probes, WIDE), lambda c, *_: (0, 0, 0, 0)),
            pl.BlockSpec((half, high, probes, WIDE), lambda c, *_: (0, 0, 0, 0)),
        ],
        scratch_shapes=[pltpu.VMEM((leaf_count, high, probes, WIDE), jnp.float32)],
    )
    return pl.pallas_call(
        sample_kernel,
        grid_spec=grid_spec,
        out_shape=[
            jax.ShapeDtypeStruct((half, high, probes, WIDE), jnp.bfloat16),
            jax.ShapeDtypeStruct((half, high, probes, WIDE), jnp.float32),
        ],
        compiler_params=pltpu.CompilerParams(vmem_limit_bytes=56 * 1024 * 1024),
    )(child_dest.reshape(-1), coupling.reshape(-1), child_updates, child_probes, rows,
      parent_blocks, parent_probes)


def halve(values, index, bits):
    rest = list(bits)
    for bit in bits:
        ordered = sorted(rest, reverse=True)
        spot = ordered.index(bit)
        mine = index // (1 << bit) % 2
        kept = lax.dynamic_index_in_dim(values, mine, spot, keepdims=False)
        sent = lax.dynamic_index_in_dim(values, 1 - mine, spot, keepdims=False)
        came = partner_of(sent.astype(jnp.bfloat16), "leaf", bit)
        values = kept + came.astype(jnp.float32)
        rest.remove(bit)
    return values


def inverse_factor(work_u, work_v, done, gram):
    n = gram.shape[0]
    eye = lax.broadcasted_iota(jnp.int32, (n, n), 0) == lax.broadcasted_iota(jnp.int32, (n, n), 1)
    work_u[...] = gram
    work_v[...] = jnp.where(eye, 1.0, 0.0)
    place = lax.broadcasted_iota(jnp.int32, (PANEL, n), 0)
    for k in range(0, n, PANEL):
        left = work_u[k : k + PANEL, :]
        right = work_v[k : k + PANEL, :]
        for j in range(PANEL):
            column = jnp.broadcast_to(left[:, k + j : k + j + 1], (PANEL, n))
            scale = lax.rsqrt(column[j : j + 1, :])
            row_u = left[j : j + 1, :] * scale
            row_v = right[j : j + 1, :] * scale
            weight = jnp.where(place > j, column * scale, 0.0)
            left = jnp.where(place == j, row_u, left - weight * row_u)
            right = jnp.where(place == j, row_v, right - weight * row_v)
        done[k : k + PANEL, :] = right
        if k + PANEL < n:
            work_u[...] -= dot(left, left, 0, 0, highest)
            work_v[...] -= dot(left, right, 0, 0, highest)
    return done[...]


def limited(stack, inverse, rank):
    result = dot(stack, inverse, 1, 1, highest)
    columns = lax.broadcasted_iota(jnp.int32, result.shape, 1)
    return jnp.where(columns < rank, result, 0.0)


def front_kernel(rank_ref, sums_ref, sketched_ref, basis_ref, passed_ref, work_u, work_v, done):
    n = done.shape[0]
    inverse = inverse_factor(work_u, work_v, done, sums_ref[:n])
    passed_ref[...] = limited(sums_ref[n:], inverse, rank_ref[0])
    basis_ref[...] = limited(sketched_ref[...], inverse, rank_ref[0])


def merge_kernel(stride, rank_ref, own_ref, partner_ref, sketch_ref, basis_ref, passed_ref,
                 work_u, work_v, done):
    leaf = lax.axis_index("leaf")
    bit = leaf // (1 << stride) % 2
    rank = rank_ref[leaf // (2 << stride)]
    n = done.shape[0]
    own = own_ref[...]
    partner = partner_ref[...]
    stacked = jnp.concatenate(
        [jnp.where(bit == 0, own, partner), jnp.where(bit == 0, partner, own)], 1
    )
    sketched = dot(stacked, sketch_ref[...], 0, 0, highest)
    gram = dot(sketched, sketched, 0, 0, highest)
    crossed = dot(stacked, sketched, 1, 0, highest)
    inverse = inverse_factor(work_u, work_v, done, gram)
    passed_ref[...] = limited(crossed, inverse, rank)
    basis_ref[...] = limited(jnp.where(bit == 0, sketched[:n], sketched[n:]), inverse, rank)


def basis_call(kernel, outs, n, *operands):
    return pl.pallas_call(
        kernel,
        in_specs=[pl.BlockSpec(memory_space=pltpu.SMEM)]
        + [pl.BlockSpec(memory_space=pltpu.VMEM)] * (len(operands) - 1),
        out_specs=[pl.BlockSpec(memory_space=pltpu.VMEM)] * len(outs),
        out_shape=[jax.ShapeDtypeStruct(shape, jnp.float32) for shape in outs],
        scratch_shapes=[pltpu.VMEM((n, n), jnp.float32)] * 3,
        compiler_params=pltpu.CompilerParams(vmem_limit_bytes=24 * 1024 * 1024),
    )(*operands)


def merge(passed, stride, sketch, ranks):
    n = sketch.shape[1]
    partner = partner_of(passed, "leaf", stride)
    return basis_call(
        functools.partial(merge_kernel, stride), [(n, n), passed.shape], n,
        ranks, passed, partner, sketch,
    )


def on_device(
    child_updates,
    child_probes,
    child_dest,
    child_rows,
    parent_blocks,
    coupling,
    parent_probes,
    sketch,
    rank_one,
    rank_two,
    rank_three,
):
    leaf_count = lax.axis_size("leaf")
    probe_count = lax.axis_size("probe")
    leaf_index = lax.axis_index("leaf")
    probe_index = lax.axis_index("probe")
    probes, front_rows = parent_probes.shape
    rank_width = sketch.shape[1]
    high = front_rows // WIDE
    sketch_all = gathered(sketch, "probe")
    send, keep = local_samples(
        child_updates, child_probes, child_dest, child_rows, parent_blocks, coupling,
        parent_probes, leaf_count,
    )
    bits = leaf_count.bit_length() - 1
    summed = keep + partner_of(send, "leaf", 0).astype(jnp.float32)
    summed = summed.reshape((2,) * (bits - 1) + keep.shape[1:])
    rising = list(range(1, bits))
    cut = [slice(None)] * (bits - 1)
    halves = [
        halve(summed[tuple(cut + [slice(0, high // 2)])], leaf_index, rising),
        halve(summed[tuple(cut + [slice(high // 2, high)])], leaf_index, rising[::-1]),
    ]
    sample = jnp.concatenate(halves, 0)
    share = sample.astype(jnp.bfloat16).reshape(probe_count, high // probe_count, probes, WIDE)
    share = lax.all_to_all(share, "probe", 0, 0, tiled=True)
    rows_mine = jnp.moveaxis(share, 1, 2).reshape(probe_count * probes, front_rows // probe_count)
    rows_mine = rows_mine.astype(jnp.float32)
    sketched = jnp.einsum("pr,ps->rs", rows_mine, sketch_all, precision=highest)
    gram = jnp.einsum("ra,rb->ab", sketched, sketched, precision=highest)
    crossed = jnp.dot(rows_mine, sketched, precision=highest)
    sums = jnp.concatenate([gram, crossed], 0)
    stride = 0
    while 1 << stride < probe_count:
        sums = sums + partner_of(sums, "probe", stride)
        stride += 1
    own_basis, passed_one = basis_call(
        front_kernel, [sketched.shape, crossed.shape], rank_width, rank_one, sums, sketched
    )
    basis_two, passed_two = merge(passed_one, 0, sketch_all, rank_two)
    basis_three, passed_three = merge(passed_two, 1, sketch_all, rank_three)
    top = lax.dynamic_slice_in_dim(passed_three, probe_index * probes, probes, 0)
    return (own_basis, basis_two, basis_three, top)


def solution(mesh):
    return jax.shard_map(
        on_device,
        mesh=mesh,
        in_specs=(
            P("leaf", None, None),
            P("probe", "leaf"),
            P("leaf", None),
            P("leaf", None),
            P("leaf", None, None),
            P("leaf", None),
            P("probe", "leaf"),
            P("probe", None),
            P("leaf"),
            P(),
            P(),
        ),
        out_specs=(
            P(("leaf", "probe"), None),
            P("leaf", None),
            P("leaf", None),
            P("probe", "leaf"),
        ),
        check_vma=False,
    )
```

```python
import functools
import jax
import jax.numpy as jnp
from jax import lax
from jax.experimental import pallas as pl
from jax.experimental.pallas import tpu as pltpu
from jax.sharding import PartitionSpec as P

highest = lax.Precision.HIGHEST
WIDE = 256
PANEL = 32
KIDS = 2


def dot(a, b, ca, cb, precision=None):
    return lax.dot_general(
        a, b, (((ca,), (cb,)), ((), ())), precision=precision, preferred_element_type=jnp.float32
    )


def partner_of(block, axis, stride):
    count = lax.axis_size(axis)
    route = [(i, i ^ (1 << stride)) for i in range(count)]
    return lax.ppermute(block, axis, route)


def gathered(block, axis):
    count = lax.axis_size(axis)
    index = lax.axis_index(axis)
    rows = block.shape[0]
    result = jnp.zeros((count * rows,) + block.shape[1:], block.dtype)
    result = lax.dynamic_update_slice_in_dim(result, block, index * rows, 0)
    for shift in range(1, count):
        came = lax.ppermute(block, axis, [(i, (i + shift) % count) for i in range(count)])
        source = (index - shift + count) % count
        result = lax.dynamic_update_slice_in_dim(result, came, source * rows, 0)
    return result


def sample_kernel(dest_ref, coup_ref, upd_ref, probe_ref, rows_ref, blk_ref, pp_ref,
                  send_ref, keep_ref, acc):
    step = pl.program_id(0)
    me = lax.axis_index("leaf")
    high_count = acc.shape[1]
    kids, row_blocks, width = rows_ref.shape
    order = upd_ref.shape[1]

    @pl.when(step == 0)
    def _():
        acc[...] = jnp.zeros_like(acc)

    spots = lax.broadcasted_iota(jnp.int32, (WIDE, width), 0)
    sampled = [
        dot(probe_ref[:, c * order : (c + 1) * order], upd_ref[c], 1, 1).astype(jnp.bfloat16)
        for c in range(kids)
    ]
    for c in range(kids):
        for b in range(row_blocks):
            rows = rows_ref[c, b : b + 1, :]
            high = lax.shift_right_logical(rows, 8)
            low = lax.bitwise_and(rows, WIDE - 1)
            low_hot = jnp.where(spots == low, 1.0, 0.0).astype(jnp.bfloat16)
            part = sampled[c][:, b * width : (b + 1) * width]
            left = jnp.concatenate(
                [
                    part * jnp.where(high == h, 1.0, 0.0).astype(jnp.bfloat16)
                    for h in range(high_count)
                ],
                0,
            )
            spread = dot(left, low_hot, 1, 1).reshape(acc.shape[1:])
            f = dest_ref[(step * kids + c) * row_blocks + b]
            acc[f] += spread
    per_step = blk_ref.shape[0]
    for e in range(per_step):
        q = coup_ref[2 * (step * per_step + e)]
        s = coup_ref[2 * (step * per_step + e) + 1]
        picked = pp_ref[:, pl.ds(pl.multiple_of(s * width, width), width)]
        lane = pl.multiple_of((q % 2) * width, width)
        acc[me, q // 2, :, pl.ds(lane, width)] += dot(picked, blk_ref[e], 1, 1)

    @pl.when(step == pl.num_programs(0) - 1)
    def _():
        bit = me % 2
        for i in range(send_ref.shape[0]):
            send_ref[i] = acc[2 * i + 1 - bit].astype(jnp.bfloat16)
            keep_ref[i] = acc[2 * i + bit]


def local_samples(child_updates, child_probes, child_dest, child_rows, parent_blocks, coupling,
                  parent_probes, leaf_count):
    kids, order, _ = child_updates.shape
    probes = child_probes.shape[0]
    width = child_rows.shape[1]
    per_kid = order // width
    front_rows = parent_probes.shape[1]
    steps = kids // KIDS
    entries = parent_blocks.shape[0] // steps
    high = front_rows // WIDE
    half = leaf_count // 2
    rows = child_rows.reshape(kids, per_kid, width)
    grid_spec = pltpu.PrefetchScalarGridSpec(
        num_scalar_prefetch=2,
        grid=(steps,),
        in_specs=[
            pl.BlockSpec((KIDS, order, order), lambda c, *_: (c, 0, 0)),
            pl.BlockSpec((probes, KIDS * order), lambda c, *_: (0, c)),
            pl.BlockSpec((KIDS, per_kid, width), lambda c, *_: (c, 0, 0)),
            pl.BlockSpec((entries, width, width), lambda c, *_: (c, 0, 0)),
            pl.BlockSpec((probes, front_rows), lambda c, *_: (0, 0)),
        ],
        out_specs=[
            pl.BlockSpec((half, high, probes, WIDE), lambda c, *_: (0, 0, 0, 0)),
            pl.BlockSpec((half, high, probes, WIDE), lambda c, *_: (0, 0, 0, 0)),
        ],
        scratch_shapes=[pltpu.VMEM((leaf_count, high, probes, WIDE), jnp.float32)],
    )
    return pl.pallas_call(
        sample_kernel,
        grid_spec=grid_spec,
        out_shape=[
            jax.ShapeDtypeStruct((half, high, probes, WIDE), jnp.bfloat16),
            jax.ShapeDtypeStruct((half, high, probes, WIDE), jnp.float32),
        ],
        compiler_params=pltpu.CompilerParams(vmem_limit_bytes=56 * 1024 * 1024),
    )(child_dest.reshape(-1), coupling.reshape(-1), child_updates, child_probes, rows,
      parent_blocks, parent_probes)


def halve(values, index, bits):
    rest = list(bits)
    for bit in bits:
        ordered = sorted(rest, reverse=True)
        spot = ordered.index(bit)
        mine = index // (1 << bit) % 2
        kept = lax.dynamic_index_in_dim(values, mine, spot, keepdims=False)
        sent = lax.dynamic_index_in_dim(values, 1 - mine, spot, keepdims=False)
        came = partner_of(sent.astype(jnp.bfloat16), "leaf", bit)
        values = kept + came.astype(jnp.float32)
        rest.remove(bit)
    return values


def inverse_factor(work_u, work_v, done, gram):
    n = gram.shape[0]
    eye = lax.broadcasted_iota(jnp.int32, (n, n), 0) == lax.broadcasted_iota(jnp.int32, (n, n), 1)
    work_u[...] = gram
    work_v[...] = jnp.where(eye, 1.0, 0.0)
    place = lax.broadcasted_iota(jnp.int32, (PANEL, n), 0)
    for k in range(0, n, PANEL):
        left = work_u[k : k + PANEL, :]
        right = work_v[k : k + PANEL, :]
        for j in range(PANEL):
            column = jnp.broadcast_to(left[:, k + j : k + j + 1], (PANEL, n))
            scale = lax.rsqrt(column[j : j + 1, :])
            row_u = left[j : j + 1, :] * scale
            row_v = right[j : j + 1, :] * scale
            weight = jnp.where(place > j, column * scale, 0.0)
            left = jnp.where(place == j, row_u, left - weight * row_u)
            right = jnp.where(place == j, row_v, right - weight * row_v)
        done[k : k + PANEL, :] = right
        if k + PANEL < n:
            work_u[...] -= dot(left, left, 0, 0, highest)
            work_v[...] -= dot(left, right, 0, 0, highest)
    return done[...]


def limited(stack, inverse, rank):
    result = dot(stack, inverse, 1, 1, highest)
    columns = lax.broadcasted_iota(jnp.int32, result.shape, 1)
    return jnp.where(columns < rank, result, 0.0)


def front_kernel(rank_ref, sums_ref, sketched_ref, basis_ref, passed_ref, work_u, work_v, done):
    n = done.shape[0]
    inverse = inverse_factor(work_u, work_v, done, sums_ref[:n])
    passed_ref[...] = limited(sums_ref[n:], inverse, rank_ref[0])
    basis_ref[...] = limited(sketched_ref[...], inverse, rank_ref[0])


def merge_kernel(stride, rank_ref, own_ref, partner_ref, sketch_ref, basis_ref, passed_ref,
                 work_u, work_v, done):
    leaf = lax.axis_index("leaf")
    bit = leaf // (1 << stride) % 2
    rank = rank_ref[leaf // (2 << stride)]
    n = done.shape[0]
    own = own_ref[...]
    partner = partner_ref[...]
    stacked = jnp.concatenate(
        [jnp.where(bit == 0, own, partner), jnp.where(bit == 0, partner, own)], 1
    )
    sketched = dot(stacked, sketch_ref[...], 0, 0, highest)
    gram = dot(sketched, sketched, 0, 0, highest)
    crossed = dot(stacked, sketched, 1, 0, highest)
    inverse = inverse_factor(work_u, work_v, done, gram)
    passed_ref[...] = limited(crossed, inverse, rank)
    basis_ref[...] = limited(jnp.where(bit == 0, sketched[:n], sketched[n:]), inverse, rank)


def basis_call(kernel, outs, n, *operands):
    return pl.pallas_call(
        kernel,
        in_specs=[pl.BlockSpec(memory_space=pltpu.SMEM)]
        + [pl.BlockSpec(memory_space=pltpu.VMEM)] * (len(operands) - 1),
        out_specs=[pl.BlockSpec(memory_space=pltpu.VMEM)] * len(outs),
        out_shape=[jax.ShapeDtypeStruct(shape, jnp.float32) for shape in outs],
        scratch_shapes=[pltpu.VMEM((n, n), jnp.float32)] * 3,
        compiler_params=pltpu.CompilerParams(vmem_limit_bytes=24 * 1024 * 1024),
    )(*operands)


def merge(passed, stride, sketch, ranks):
    n = sketch.shape[1]
    partner = partner_of(passed, "leaf", stride)
    return basis_call(
        functools.partial(merge_kernel, stride), [(n, n), passed.shape], n,
        ranks, passed, partner, sketch,
    )


def on_device(
    child_updates,
    child_probes,
    child_dest,
    child_rows,
    parent_blocks,
    coupling,
    parent_probes,
    sketch,
    rank_one,
    rank_two,
    rank_three,
):
    leaf_count = lax.axis_size("leaf")
    probe_count = lax.axis_size("probe")
    leaf_index = lax.axis_index("leaf")
    probe_index = lax.axis_index("probe")
    probes, front_rows = parent_probes.shape
    rank_width = sketch.shape[1]
    high = front_rows // WIDE
    sketch_all = gathered(sketch, "probe")
    send, keep = local_samples(
        child_updates, child_probes, child_dest, child_rows, parent_blocks, coupling,
        parent_probes, leaf_count,
    )
    bits = leaf_count.bit_length() - 1
    summed = keep + partner_of(send, "leaf", 0).astype(jnp.float32)
    summed = summed.reshape((2,) * (bits - 1) + keep.shape[1:])
    rising = list(range(1, bits))
    cut = [slice(None)] * (bits - 1)
    halves = [
        halve(summed[tuple(cut + [slice(0, high // 2)])], leaf_index, rising),
        halve(summed[tuple(cut + [slice(high // 2, high)])], leaf_index, rising[::-1]),
    ]
    sample = jnp.concatenate(halves, 0)
    share = sample.astype(jnp.bfloat16).reshape(probe_count, high // probe_count, probes, WIDE)
    share = lax.all_to_all(share, "probe", 0, 0, tiled=True)
    rows_mine = jnp.moveaxis(share, 1, 2).reshape(probe_count * probes, front_rows // probe_count)
    rows_mine = rows_mine.astype(jnp.float32)
    sketched = jnp.einsum("pr,ps->rs", rows_mine, sketch_all, precision=highest)
    gram = jnp.einsum("ra,rb->ab", sketched, sketched, precision=highest)
    crossed = jnp.dot(rows_mine, sketched, precision=highest)
    sums = jnp.concatenate([gram, crossed], 0)
    stride = 0
    while 1 << stride < probe_count:
        sums = sums + partner_of(sums, "probe", stride)
        stride += 1
    own_basis, passed_one = basis_call(
        front_kernel, [sketched.shape, crossed.shape], rank_width, rank_one, sums, sketched
    )
    basis_two, passed_two = merge(passed_one, 0, sketch_all, rank_two)
    basis_three, passed_three = merge(passed_two, 1, sketch_all, rank_three)
    top = lax.dynamic_slice_in_dim(passed_three, probe_index * probes, probes, 0)
    return (own_basis, basis_two, basis_three, top)


def solution(mesh):
    return jax.shard_map(
        on_device,
        mesh=mesh,
        in_specs=(
            P("leaf", None, None),
            P("probe", "leaf"),
            P("leaf", None),
            P("leaf", None),
            P("leaf", None, None),
            P("leaf", None),
            P("probe", "leaf"),
            P("probe", None),
            P("leaf"),
            P(),
            P(),
        ),
        out_specs=(
            P(("leaf", "probe"), None),
            P("leaf", None),
            P("leaf", None),
            P("probe", "leaf"),
        ),
        check_vma=False,
    )
```

```python
import functools
import jax
import jax.numpy as jnp
from jax import lax
from jax.experimental import pallas as pl
from jax.experimental.pallas import tpu as pltpu
from jax.sharding import PartitionSpec as P

highest = lax.Precision.HIGHEST
WIDE = 256
PANEL = 32
KIDS = 2


def dot(a, b, ca, cb, precision=None):
    return lax.dot_general(
        a, b, (((ca,), (cb,)), ((), ())), precision=precision, preferred_element_type=jnp.float32
    )


def partner_of(block, axis, stride):
    count = lax.axis_size(axis)
    route = [(i, i ^ (1 << stride)) for i in range(count)]
    return lax.ppermute(block, axis, route)


def gathered(block, axis):
    count = lax.axis_size(axis)
    index = lax.axis_index(axis)
    rows = block.shape[0]
    result = jnp.zeros((count * rows,) + block.shape[1:], block.dtype)
    result = lax.dynamic_update_slice_in_dim(result, block, index * rows, 0)
    for shift in range(1, count):
        came = lax.ppermute(block, axis, [(i, (i + shift) % count) for i in range(count)])
        source = (index - shift + count) % count
        result = lax.dynamic_update_slice_in_dim(result, came, source * rows, 0)
    return result


def sample_kernel(dest_ref, coup_ref, upd_ref, probe_ref, rows_ref, blk_ref, pp_ref,
                  send_ref, keep_ref, acc):
    step = pl.program_id(0)
    me = lax.axis_index("leaf")
    high_count = acc.shape[1]
    kids, row_blocks, width = rows_ref.shape
    order = upd_ref.shape[1]

    @pl.when(step == 0)
    def _():
        acc[...] = jnp.zeros_like(acc)

    spots = lax.broadcasted_iota(jnp.int32, (WIDE, width), 0)
    sampled = [
        dot(probe_ref[:, c * order : (c + 1) * order], upd_ref[c], 1, 1).astype(jnp.bfloat16)
        for c in range(kids)
    ]
    for c in range(kids):
        for b in range(row_blocks):
            rows = rows_ref[c, b : b + 1, :]
            high = lax.shift_right_logical(rows, 8)
            low = lax.bitwise_and(rows, WIDE - 1)
            low_hot = jnp.where(spots == low, 1.0, 0.0).astype(jnp.bfloat16)
            part = sampled[c][:, b * width : (b + 1) * width]
            left = jnp.concatenate(
                [
                    part * jnp.where(high == h, 1.0, 0.0).astype(jnp.bfloat16)
                    for h in range(high_count)
                ],
                0,
            )
            spread = dot(left, low_hot, 1, 1).reshape(acc.shape[1:])
            f = dest_ref[(step * kids + c) * row_blocks + b]
            acc[f] += spread
    per_step = blk_ref.shape[0]
    for e in range(per_step):
        q = coup_ref[2 * (step * per_step + e)]
        s = coup_ref[2 * (step * per_step + e) + 1]
        picked = pp_ref[:, pl.ds(pl.multiple_of(s * width, width), width)]
        lane = pl.multiple_of((q % 2) * width, width)
        acc[me, q // 2, :, pl.ds(lane, width)] += dot(picked, blk_ref[e], 1, 1)

    @pl.when(step == pl.num_programs(0) - 1)
    def _():
        bit = me % 2
        for i in range(send_ref.shape[0]):
            send_ref[i] = acc[2 * i + 1 - bit].astype(jnp.bfloat16)
            keep_ref[i] = acc[2 * i + bit]


def local_samples(child_updates, child_probes, child_dest, child_rows, parent_blocks, coupling,
                  parent_probes, leaf_count):
    kids, order, _ = child_updates.shape
    probes = child_probes.shape[0]
    width = child_rows.shape[1]
    per_kid = order // width
    front_rows = parent_probes.shape[1]
    steps = kids // KIDS
    entries = parent_blocks.shape[0] // steps
    high = front_rows // WIDE
    half = leaf_count // 2
    rows = child_rows.reshape(kids, per_kid, width)
    grid_spec = pltpu.PrefetchScalarGridSpec(
        num_scalar_prefetch=2,
        grid=(steps,),
        in_specs=[
            pl.BlockSpec((KIDS, order, order), lambda c, *_: (c, 0, 0)),
            pl.BlockSpec((probes, KIDS * order), lambda c, *_: (0, c)),
            pl.BlockSpec((KIDS, per_kid, width), lambda c, *_: (c, 0, 0)),
            pl.BlockSpec((entries, width, width), lambda c, *_: (c, 0, 0)),
            pl.BlockSpec((probes, front_rows), lambda c, *_: (0, 0)),
        ],
        out_specs=[
            pl.BlockSpec((half, high, probes, WIDE), lambda c, *_: (0, 0, 0, 0)),
            pl.BlockSpec((half, high, probes, WIDE), lambda c, *_: (0, 0, 0, 0)),
        ],
        scratch_shapes=[pltpu.VMEM((leaf_count, high, probes, WIDE), jnp.float32)],
    )
    return pl.pallas_call(
        sample_kernel,
        grid_spec=grid_spec,
        out_shape=[
            jax.ShapeDtypeStruct((half, high, probes, WIDE), jnp.bfloat16),
            jax.ShapeDtypeStruct((half, high, probes, WIDE), jnp.float32),
        ],
        compiler_params=pltpu.CompilerParams(vmem_limit_bytes=56 * 1024 * 1024),
        cost_estimate=pl.CostEstimate(
            flops=20 * 10**9, bytes_accessed=child_updates.size * 2, transcendentals=0
        ),
    )(child_dest.reshape(-1), coupling.reshape(-1), child_updates, child_probes, rows,
      parent_blocks, parent_probes)


def halve(values, index, bits):
    rest = list(bits)
    for bit in bits:
        ordered = sorted(rest, reverse=True)
        spot = ordered.index(bit)
        mine = index // (1 << bit) % 2
        kept = lax.dynamic_index_in_dim(values, mine, spot, keepdims=False)
        sent = lax.dynamic_index_in_dim(values, 1 - mine, spot, keepdims=False)
        came = partner_of(sent.astype(jnp.bfloat16), "leaf", bit)
        values = kept + came.astype(jnp.float32)
        rest.remove(bit)
    return values


def inverse_factor(work_u, work_v, done, gram):
    n = gram.shape[0]
    eye = lax.broadcasted_iota(jnp.int32, (n, n), 0) == lax.broadcasted_iota(jnp.int32, (n, n), 1)
    work_u[...] = gram
    work_v[...] = jnp.where(eye, 1.0, 0.0)
    place = lax.broadcasted_iota(jnp.int32, (PANEL, n), 0)
    for k in range(0, n, PANEL):
        left = work_u[k : k + PANEL, :]
        right = work_v[k : k + PANEL, :]
        for j in range(PANEL):
            column = jnp.broadcast_to(left[:, k + j : k + j + 1], (PANEL, n))
            scale = lax.rsqrt(column[j : j + 1, :])
            row_u = left[j : j + 1, :] * scale
            row_v = right[j : j + 1, :] * scale
            weight = jnp.where(place > j, column * scale, 0.0)
            left = jnp.where(place == j, row_u, left - weight * row_u)
            right = jnp.where(place == j, row_v, right - weight * row_v)
        done[k : k + PANEL, :] = right
        if k + PANEL < n:
            work_u[...] -= dot(left, left, 0, 0, highest)
            work_v[...] -= dot(left, right, 0, 0, highest)
    return done[...]


def limited(stack, inverse, rank):
    result = dot(stack, inverse, 1, 1, highest)
    columns = lax.broadcasted_iota(jnp.int32, result.shape, 1)
    return jnp.where(columns < rank, result, 0.0)


def front_kernel(rank_ref, gram_ref, sketched_ref, basis_ref, inverse_ref, work_u, work_v, done):
    inverse = inverse_factor(work_u, work_v, done, gram_ref[...])
    inverse_ref[...] = inverse
    basis_ref[...] = limited(sketched_ref[...], inverse, rank_ref[0])


def merge_kernel(stride, rank_ref, own_ref, partner_ref, sketch_ref, basis_ref, passed_ref,
                 work_u, work_v, done):
    leaf = lax.axis_index("leaf")
    bit = leaf // (1 << stride) % 2
    rank = rank_ref[leaf // (2 << stride)]
    n = done.shape[0]
    own = own_ref[...]
    partner = partner_ref[...]
    stacked = jnp.concatenate(
        [jnp.where(bit == 0, own, partner), jnp.where(bit == 0, partner, own)], 1
    )
    sketched = dot(stacked, sketch_ref[...], 0, 0, highest)
    gram = dot(sketched, sketched, 0, 0, highest)
    crossed = dot(stacked, sketched, 1, 0, highest)
    inverse = inverse_factor(work_u, work_v, done, gram)
    passed_ref[...] = limited(crossed, inverse, rank)
    basis_ref[...] = limited(jnp.where(bit == 0, sketched[:n], sketched[n:]), inverse, rank)


def basis_call(kernel, outs, n, *operands):
    return pl.pallas_call(
        kernel,
        in_specs=[pl.BlockSpec(memory_space=pltpu.SMEM)]
        + [pl.BlockSpec(memory_space=pltpu.VMEM)] * (len(operands) - 1),
        out_specs=[pl.BlockSpec(memory_space=pltpu.VMEM)] * len(outs),
        out_shape=[jax.ShapeDtypeStruct(shape, jnp.float32) for shape in outs],
        scratch_shapes=[pltpu.VMEM((n, n), jnp.float32)] * 3,
        compiler_params=pltpu.CompilerParams(vmem_limit_bytes=24 * 1024 * 1024),
        cost_estimate=pl.CostEstimate(flops=12 * 10**9, bytes_accessed=2**19, transcendentals=n),
    )(*operands)


def merge(passed, stride, sketch, ranks):
    n = sketch.shape[1]
    partner = partner_of(passed, "leaf", stride)
    return basis_call(
        functools.partial(merge_kernel, stride), [(n, n), passed.shape], n,
        ranks, passed, partner, sketch,
    )


def on_device(
    child_updates,
    child_probes,
    child_dest,
    child_rows,
    parent_blocks,
    coupling,
    parent_probes,
    sketch,
    rank_one,
    rank_two,
    rank_three,
):
    leaf_count = lax.axis_size("leaf")
    probe_count = lax.axis_size("probe")
    leaf_index = lax.axis_index("leaf")
    probe_index = lax.axis_index("probe")
    probes, front_rows = parent_probes.shape
    rank_width = sketch.shape[1]
    high = front_rows // WIDE
    sketch_all = gathered(sketch, "probe")
    send, keep = local_samples(
        child_updates, child_probes, child_dest, child_rows, parent_blocks, coupling,
        parent_probes, leaf_count,
    )
    bits = leaf_count.bit_length() - 1
    summed = keep + partner_of(send, "leaf", 0).astype(jnp.float32)
    summed = summed.reshape((2,) * (bits - 1) + keep.shape[1:])
    rising = list(range(1, bits))
    cut = [slice(None)] * (bits - 1)
    halves = [
        halve(summed[tuple(cut + [slice(0, high // 2)])], leaf_index, rising),
        halve(summed[tuple(cut + [slice(high // 2, high)])], leaf_index, rising[::-1]),
    ]
    sample = jnp.concatenate(halves, 0)
    share = sample.astype(jnp.bfloat16).reshape(probe_count, high // probe_count, probes, WIDE)
    share = lax.all_to_all(share, "probe", 0, 0, tiled=True)
    rows_mine = jnp.moveaxis(share, 1, 2).reshape(probe_count * probes, front_rows // probe_count)
    rows_mine = rows_mine.astype(jnp.float32)
    sketched = jnp.einsum("pr,ps->rs", rows_mine, sketch_all, precision=highest)
    gram = jnp.einsum("ra,rb->ab", sketched, sketched, precision=highest)
    crossed = jnp.dot(rows_mine, sketched, precision=highest)
    stride = 0
    while 1 << stride < probe_count:
        gram = gram + partner_of(gram, "probe", stride)
        crossed = crossed + partner_of(crossed, "probe", stride)
        stride += 1
    own_basis, inverse = basis_call(
        front_kernel, [sketched.shape, gram.shape], rank_width, rank_one, gram, sketched
    )
    passed_one = jnp.einsum("pr,sr->ps", crossed, inverse, precision=highest)
    passed_one = jnp.where(jnp.arange(rank_width)[None, :] < rank_one[0], passed_one, 0.0)
    basis_two, passed_two = merge(passed_one, 0, sketch_all, rank_two)
    basis_three, passed_three = merge(passed_two, 1, sketch_all, rank_three)
    top = lax.dynamic_slice_in_dim(passed_three, probe_index * probes, probes, 0)
    return (own_basis, basis_two, basis_three, top)


def solution(mesh):
    return jax.shard_map(
        on_device,
        mesh=mesh,
        in_specs=(
            P("leaf", None, None),
            P("probe", "leaf"),
            P("leaf", None),
            P("leaf", None),
            P("leaf", None, None),
            P("leaf", None),
            P("probe", "leaf"),
            P("probe", None),
            P("leaf"),
            P(),
            P(),
        ),
        out_specs=(
            P(("leaf", "probe"), None),
            P("leaf", None),
            P("leaf", None),
            P("probe", "leaf"),
        ),
        check_vma=False,
    )
```
